128 devices in a mesh: section: 4 (over y_lo, core), row: 4 (over x), col: 8 (over y_hi, z).
Axes of the slice: x: 4, y: 4 (y_hi: 2, y_lo: 2; y = y_hi * 2 + y_lo), z: 4, core: 2. Of those that a mesh axis runs over, the one named last changes fastest.
Arguments:
- inputs: bfloat16 [4, 1024, 6144], P('section', 'col', 'row'), may hold values from -450 to 450
- cotangent: bfloat16 [4, 1024, 6144], P('section', 'col', 'row'), may hold values from -2 to 2
- stashed: bfloat16 [4, 1024, 12288], P('section', 'row', 'col'), may hold values from -6 to 6
- weight_in: bfloat16 [4, 6144, 12288], P('section', 'row', 'col'), may hold values from -0.078125 to 0.078125
- weight_out: bfloat16 [4, 12288, 6144], P('section', 'col', 'row'), may hold values from -0.0546875 to 0.0546875
- norm_gain: float32 [4, 6144], P('section', 'row'), may hold values from 0.3 to 8
Outputs:
- grad_in: bfloat16 [4, 6144, 12288], P('section', 'row', 'col')
- grad_out: bfloat16 [4, 12288, 6144], P('section', 'col', 'row')
- grad_gain: float32 [4, 6144], P('section', 'row')
- passed: bfloat16 [4, 1024, 6144], P('section', 'col', 'row')
The draws below stay inside these ranges and needn't reach their ends.
All inputs are finite; a program needn't handle non-finite values.
Results may differ from the reference program's by a relative error of at most 0.0015.
The reference program's roundings to bfloat16 on the way count: a program that leaves them out, or rounds other values in their place, can miss the bound.
Values may be sent and summed in bfloat16 or wider, within the bound.
No kernel may reach another device: no remote copies, remote signals or barrier semaphores. Data moves between devices by JAX's collectives and lax.ppermute only.
A program may use at most 128 MiB of HBM per device.

```python
import math
import jax
import jax.numpy as jnp
from jax import lax

D = 6144
FF = 12288
TOKENS = 1024
SECTIONS = 4


def draw_inputs(key, part):
    key = jax.random.fold_in(key, 11)
    first, second, third = jax.random.split(key, 3)
    base = jnp.clip(jax.random.normal(first, (SECTIONS, TOKENS, D), jnp.float32), -4.0, 4.0)
    row_scale = jnp.exp(jax.random.uniform(second, (SECTIONS, TOKENS, 1), jnp.float32) * math.log(10.0))
    column_scale = jnp.exp(jax.random.uniform(third, (SECTIONS, 1, D), jnp.float32) * math.log(10.0))
    return (base * row_scale * column_scale).astype(jnp.bfloat16)


def gain_ramp(key, low, ratio, rough):
    position = jnp.arange(D, dtype=jnp.float32) / (D - 1)
    ramp = low * jnp.exp(position * math.log(ratio))
    jitter = jnp.exp(jax.random.uniform(key, (SECTIONS, D), jnp.float32, -rough, rough))
    return ramp[None, :] * jitter


def draw_norm_gain(key, part):
    key = jax.random.fold_in(key, 23)
    values = gain_ramp(key, 0.6, 6.0, 0.25)
    return values.astype(jnp.float32)


def block_levels(stream_key, dims, cuts, least, high):
    def one(axis_at, blocks):
        heights = jax.random.uniform(jax.random.fold_in(jax.random.fold_in(stream_key, 6), axis_at), (blocks,), jnp.float32, least / len(cuts), high / len(cuts))
        return jnp.repeat(jnp.exp(heights), dims[axis_at] // blocks).reshape((-1,) + (1,) * (len(dims) - axis_at - 1))

    level = one(*cuts[0])
    for cut in cuts[1:]:
        level = level * one(*cut)
    return level


def centred(rng, dims, deviation, reach, cuts=(), kind=jnp.bfloat16):
    entries = deviation * jax.random.normal(rng, dims, jnp.float32)
    if cuts:
        entries = entries * block_levels(rng, dims, cuts, -0.22, 0.18)
    return jnp.clip(entries, -reach, reach).astype(kind)


def setup_inputs(seed: int = 0) -> dict:
    splits = jax.random.split(jax.random.key(seed), 7)
    inputs = draw_inputs(jax.random.fold_in(splits[6], 71), 0)
    cotangent = centred(splits[1], (SECTIONS, TOKENS, D), 0.25, 2.0, ((0, 4), (1, 8), (2, 4)))
    stashed = centred(splits[2], (SECTIONS, TOKENS, FF), 1.5, 6.0, ((0, 4), (1, 4), (2, 8)))
    weight_in = centred(splits[3], (SECTIONS, D, FF), D ** -0.5, 0.078125, ((0, 4), (1, 4), (2, 8)))
    weight_out = centred(splits[4], (SECTIONS, FF, D), FF ** -0.5, 0.0546875, ((0, 4), (1, 8), (2, 4)))
    norm_gain = draw_norm_gain(jax.random.fold_in(splits[6], 71), 0)
    return dict(inputs=inputs, cotangent=cotangent, stashed=stashed, weight_in=weight_in, weight_out=weight_out, norm_gain=norm_gain)


epsilon = 1e-06
half_root = 0.7071067811865476
density_factor = 0.3989422804014327

def gelu_parts(values):
    cumulative = 0.5 * (1.0 + lax.erf(values * half_root))
    density = jnp.exp(-0.5 * values * values) * density_factor
    return (values * cumulative, cumulative + values * density)

def times_trans(left, right):
    return lax.dot_general(left, right, (((1,), (1,)), ((), ())), preferred_element_type=jnp.float32)

def trans_times(left, right):
    return lax.dot_general(left, right, (((0,), (0,)), ((), ())), preferred_element_type=jnp.float32)

def reference(inputs, cotangent, stashed, weight_in, weight_out, norm_gain):
    grads_in = []
    grads_out = []
    grads_gain = []
    input_grads = []
    for section_index in range(SECTIONS):
        values = inputs[section_index].astype(jnp.float32)
        average = lax.optimization_barrier(jnp.sum(values, axis=1)) / D
        spread = lax.optimization_barrier(jnp.sum(values * values, axis=1)) / D - average * average
        inv_scale = lax.rsqrt(spread + epsilon)
        standard = (values - average[:, None]) * inv_scale[:, None]
        gains = norm_gain[section_index]
        normed = (standard * gains).astype(jnp.bfloat16)
        activated, slopes = gelu_parts(stashed[section_index].astype(jnp.float32))
        activated = activated.astype(jnp.bfloat16)
        upstream = cotangent[section_index]
        hidden_grad = times_trans(upstream, weight_out[section_index])
        deltas = (hidden_grad * slopes).astype(jnp.bfloat16)
        grads_out.append(trans_times(activated, upstream).astype(jnp.bfloat16))
        grads_in.append(trans_times(normed, deltas).astype(jnp.bfloat16))
        normed_grad = times_trans(deltas, weight_in[section_index])
        grads_gain.append(lax.optimization_barrier(jnp.sum(normed_grad * standard, axis=0)))
        scaled_grad = normed_grad * gains
        first_mean = lax.optimization_barrier(jnp.sum(scaled_grad, axis=1)) / D
        second_mean = lax.optimization_barrier(jnp.sum(scaled_grad * standard, axis=1)) / D
        result_grad = upstream.astype(jnp.float32) + inv_scale[:, None] * (scaled_grad - first_mean[:, None] - standard * second_mean[:, None])
        input_grads.append(result_grad.astype(jnp.bfloat16))
    input_grads.append(jnp.zeros((TOKENS, D), jnp.bfloat16))
    passed = jnp.stack(input_grads[1:])
    return (jnp.stack(grads_in), jnp.stack(grads_out), jnp.stack(grads_gain), passed)
```

```python
import functools

import jax
import jax.numpy as jnp
from jax import lax
from jax.experimental import pallas as pl
from jax.experimental.pallas import tpu as pltpu
from jax.sharding import PartitionSpec as P

epsilon = 1e-06
half_root = 0.7071067811865476
density_factor = 0.3989422804014327

chunk_rows = (64, 64)
vmem_bytes = 40 * 1024 * 1024


def along_x(block, step):
    return lax.ppermute(block, "row", [(i, (i + step) % 4) for i in range(4)])


def along_z(block, step):
    route = [(j, j // 4 * 4 + (j % 4 + step) % 4) for j in range(8)]
    return lax.ppermute(block, "col", route)


def along_y(block):
    return lax.ppermute(block, "col", [(j, (j + 4) % 8) for j in range(8)])


def to_layer_before(block):
    return lax.ppermute(block, "section", [(i, i - 1) for i in range(1, 4)])


def gelu_parts(values):
    cumulative = 0.5 * (1.0 + lax.erf(values * half_root))
    density = jnp.exp(-0.5 * values * values) * density_factor
    return (values * cumulative, cumulative + values * density)


def dot_trans(left, right):
    return lax.dot_general(
        left, right, (((1,), (1,)), ((), ())), preferred_element_type=jnp.float32
    )


def trans_dot(left, right):
    return lax.dot_general(
        left, right, (((0,), (0,)), ((), ())), preferred_element_type=jnp.float32
    )


def whole(shape):
    return pl.BlockSpec(shape, lambda n, *_: (0,) * len(shape))


def columns(rows, width):
    return pl.BlockSpec((rows, width), lambda n, *_: (0, n))


def hidden_kernel(rows, places, *refs):
    pieces, weight = refs[:8], refs[8]
    ordered, to_right, to_left, right_top, left_bottom, own = refs[9:]

    @pl.when(pl.program_id(0) == 0)
    def _():
        for place, piece in enumerate(pieces):
            start = pl.multiple_of(places[place], rows)
            ordered[pl.ds(start, rows), :] = piece[...]

    product = dot_trans(ordered[...], weight[...])
    own[...] = product[: 2 * rows]
    right_top[...] = product[2 * rows : 3 * rows]
    to_right[rows:, :] = product[3 * rows : 4 * rows]
    to_right[:rows, :] = product[4 * rows : 5 * rows]
    to_left[rows:, :] = product[5 * rows : 6 * rows]
    to_left[:rows, :] = product[6 * rows : 7 * rows]
    left_bottom[...] = product[7 * rows :]


def hidden_parts(places, pieces, weight, tile=512):
    rows, depth = pieces[0].shape
    width = weight.shape[0]
    heights = (2 * rows, 2 * rows, rows, rows, 2 * rows)
    return pl.pallas_call(
        functools.partial(hidden_kernel, rows),
        grid_spec=pltpu.PrefetchScalarGridSpec(
            num_scalar_prefetch=1,
            grid=(width // tile,),
            in_specs=[whole((rows, depth))] * 8
            + [pl.BlockSpec((tile, depth), lambda n, *_: (n, 0))],
            out_specs=[whole((8 * rows, depth))] + [columns(h, tile) for h in heights],
        ),
        out_shape=[jax.ShapeDtypeStruct((8 * rows, depth), jnp.bfloat16)]
        + [jax.ShapeDtypeStruct((h, width), jnp.float32) for h in heights],
        compiler_params=pltpu.CompilerParams(vmem_limit_bytes=vmem_bytes),
        cost_estimate=pl.CostEstimate(
            flops=16 * rows * depth * width,
            bytes_accessed=2 * width * depth + 32 * rows * depth + 32 * rows * width,
            transcendentals=0,
        ),
    )(places, *pieces, weight)


def normed_kernel(rows, places, *refs):
    own, right, far_top, far_bottom, left, weight = refs[:6]
    ordered, mine, plane, far_plane, to_up, to_down, far, up_top, down_bottom = refs[6:15]
    held = refs[15]
    half = rows // 2

    @pl.when(pl.program_id(0) == 0)
    def _():
        held[: 2 * rows, :] = own[...]
        held[2 * rows : 4 * rows, :] = right[...]
        held[4 * rows : 5 * rows, :] = far_top[...]
        held[5 * rows : 6 * rows, :] = far_bottom[...]
        held[6 * rows :, :] = left[...]
        for place in range(8):
            start = pl.multiple_of(places[place], rows)
            ordered[place * rows : (place + 1) * rows, :] = held[pl.ds(start, rows), :]

    product = dot_trans(ordered[...], weight[...])
    block = lambda place: product[place * rows : (place + 1) * rows]
    mine[...] = block(0)
    up_top[...] = block(1)[:half]
    to_up[rows:, :] = block(1)[half:]
    far[...] = block(2)
    to_down[rows:, :] = block(3)[:half]
    down_bottom[...] = block(3)[half:]
    plane[...] = block(4)
    to_up[:rows, :] = block(5)
    far_plane[...] = block(6)
    to_down[:rows, :] = block(7)


def normed_parts(places, pieces, weight, tile=512):
    rows, depth = pieces[2].shape
    width = weight.shape[0]
    half = rows // 2
    heights = (rows, rows, rows, rows + half, rows + half, rows, half, half)
    return pl.pallas_call(
        functools.partial(normed_kernel, rows),
        grid_spec=pltpu.PrefetchScalarGridSpec(
            num_scalar_prefetch=1,
            grid=(width // tile,),
            in_specs=[whole(piece.shape) for piece in pieces]
            + [pl.BlockSpec((tile, depth), lambda n, *_: (n, 0))],
            out_specs=[whole((8 * rows, depth))] + [columns(h, tile) for h in heights],
            scratch_shapes=[pltpu.VMEM((8 * rows, depth), jnp.bfloat16)],
        ),
        out_shape=[jax.ShapeDtypeStruct((8 * rows, depth), jnp.bfloat16)]
        + [jax.ShapeDtypeStruct((h, width), jnp.float32) for h in heights],
        compiler_params=pltpu.CompilerParams(vmem_limit_bytes=vmem_bytes),
        cost_estimate=pl.CostEstimate(
            flops=16 * rows * depth * width,
            bytes_accessed=2 * width * depth + 32 * rows * depth + 32 * rows * width,
            transcendentals=0,
        ),
    )(places, *pieces, weight)


def weight_kernel(cuts, sizes, *refs):
    count = len(cuts)
    pieces = refs[: len(refs) - count - 2]
    chunks, result, held = refs[len(pieces) : len(pieces) + count], refs[-2], refs[-1]
    total = None
    for chunk, cut in zip(chunks, cuts):
        at = 0
        for piece, first, rows in cut:
            held[at : at + rows, :] = pieces[piece][first : first + rows, :]
            at += rows
        term = trans_dot(held[:at, :], chunk[...])
        total = term if total is None else total + term
    result[0] = total.astype(result.dtype)


def weight_grad(pieces, cuts, chunks, tile=256):
    height = pieces[0].shape[1]
    width = chunks[0].shape[1]
    sizes = [chunk.shape[0] for chunk in chunks]
    return pl.pallas_call(
        functools.partial(weight_kernel, cuts, sizes),
        grid=(height // tile,),
        in_specs=[columns(piece.shape[0], tile) for piece in pieces]
        + [whole(chunk.shape) for chunk in chunks],
        out_specs=pl.BlockSpec((1, tile, width), lambda n: (0, n, 0)),
        out_shape=jax.ShapeDtypeStruct((1, height, width), jnp.bfloat16),
        scratch_shapes=[pltpu.VMEM((max(sizes), tile), jnp.bfloat16)],
        compiler_params=pltpu.CompilerParams(vmem_limit_bytes=vmem_bytes),
        cost_estimate=pl.CostEstimate(
            flops=2 * sum(sizes) * height * width,
            bytes_accessed=2 * (sum(sizes) * (height + width) + height * width),
            transcendentals=0,
        ),
    )(*pieces, *chunks)


def gather_col(block):
    beside = along_y(block)
    from_up, from_down = along_z(block, -1), along_z(block, 1)
    far = along_z(block, 2)
    beside_up, beside_down = along_z(beside, -1), along_z(beside, 1)
    beside_far = along_y(far)
    return [block, from_up, far, from_down, beside, beside_up, beside_far, beside_down]


def gather_row(block):
    half = block.shape[0] // 2
    from_right, from_left = along_x(block, -1), along_x(block, 1)
    far_top = along_x(from_left[:half], 1)
    far_bottom = along_x(from_right[half:], -1)
    return [block, from_right, far_top, far_bottom, from_left]


def sum_row(block):
    return (block + along_x(block, 2)) + (along_x(block, 1) + along_x(block, -1))


def sum_col(block):
    block = (block + along_z(block, 2)) + (along_z(block, 1) + along_z(block, -1))
    return block + along_y(block)


def local(inputs, cotangent, stashed, weight_in, weight_out, norm_gain):
    local_input = inputs[0]
    upstream = cotangent[0]
    hidden_pre = stashed[0]
    first_weight = weight_in[0]
    second_weight = weight_out[0]
    gains = norm_gain[0]
    width = gains.shape[0]
    feature_count = width * lax.axis_size("row")
    tokens = upstream.shape[0]
    row, col = lax.axis_index("row"), lax.axis_index("col")
    step = jnp.arange(8, dtype=jnp.int32)
    owner = (col // 4 + step // 4) % 2 * 4 + (col + step) % 4
    order = (owner // 2 - row + 4) % 4 * 2 + owner % 2

    starts, start = [], 0
    for rows in chunk_rows:
        starts.append(start)
        start += rows
    spans = list(zip(starts, chunk_rows))

    cot_pieces = [gather_col(upstream[s : s + r]) for s, r in spans]

    values = local_input.astype(jnp.float32)
    sums = jnp.stack([jnp.sum(values, axis=1), jnp.sum(values * values, axis=1)])
    sums = sum_row(sums)
    average = sums[0] / feature_count
    inv_scale = lax.rsqrt(sums[1] / feature_count - average * average + epsilon)
    standard = (values - average[:, None]) * inv_scale[:, None]
    normed_pieces = gather_col((standard * gains).astype(jnp.bfloat16))

    activated, slopes = gelu_parts(hidden_pre.astype(jnp.float32))
    activ_pieces = gather_row(activated.astype(jnp.bfloat16))

    cot_chunks, delta_chunks, received = [], [], []
    gain_part = None
    for (s, r), pieces in zip(spans, cot_pieces):
        places = order * r
        ordered, to_right, to_left, right_top, left_bottom, own = hidden_parts(
            places, pieces, second_weight
        )
        cot_chunks.append(ordered)
        from_left, from_right = along_x(to_right, 1), along_x(to_left, -1)
        top = along_x(right_top + from_left[:r], 1)
        bottom = along_x(left_bottom + from_right[r:], -1)
        top_slopes = slopes[s : s + r]
        bottom_slopes = slopes[tokens + s : tokens + s + r]
        deltas = jnp.concatenate(
            [
                ((own[:r] + from_right[:r]) + top) * top_slopes,
                ((own[r:] + from_left[r:]) + bottom) * bottom_slopes,
            ]
        ).astype(jnp.bfloat16)
        delta_pieces = gather_row(deltas)
        ordered, mine, plane, far_plane, to_up, to_down, far, up_top, down_bottom = (
            normed_parts(places, delta_pieces, first_weight)
        )
        delta_chunks.append(ordered)
        half = r // 2
        far = far + along_y(far_plane)
        from_down, from_up = along_z(to_up, 1), along_z(to_down, -1)
        plane = (plane + from_down[:r]) + from_up[:r]
        beside = along_y(plane)
        far_top, far_bottom = along_z(far[:half], 1), along_z(far[half:], -1)
        top = along_z(up_top + far_top, 1)
        bottom = along_z(down_bottom + far_bottom, -1)
        normed_grad = (mine + beside) + jnp.concatenate(
            [from_up[r:] + top, from_down[r:] + bottom]
        )
        chunk_standard = standard[s : s + r]
        part = jnp.sum(normed_grad * chunk_standard, axis=0)
        gain_part = part if gain_part is None else gain_part + part
        scaled_grad = normed_grad * gains
        means = sum_row(
            jnp.stack(
                [jnp.sum(scaled_grad, axis=1), jnp.sum(scaled_grad * chunk_standard, axis=1)]
            )
        )
        means = means / feature_count
        result_grad = upstream[s : s + r].astype(jnp.float32) + inv_scale[s : s + r, None] * (
            scaled_grad - means[0][:, None] - chunk_standard * means[1][:, None]
        )
        received.append(to_layer_before(result_grad.astype(jnp.bfloat16)))

    gain_grad = sum_col(gain_part[None])

    activ_cuts, normed_cuts = [], []
    for s, r in spans:
        activ_cuts.append(
            [
                (0, s, r),
                (0, tokens + s, r),
                (1, s, r),
                (1, tokens + s, r),
                (2, s, r),
                (3, s, r),
                (4, s, r),
                (4, tokens + s, r),
            ]
        )
        normed_cuts.append([(piece, s, r) for piece in range(8)])
    out_grad = weight_grad(activ_pieces, activ_cuts, cot_chunks)
    in_grad = weight_grad(normed_pieces, normed_cuts, delta_chunks)
    return (in_grad, out_grad, gain_grad, jnp.concatenate(received)[None])


def solution(mesh):
    return jax.shard_map(
        local,
        mesh=mesh,
        in_specs=(
            P("section", "col", "row"),
            P("section", "col", "row"),
            P("section", "row", "col"),
            P("section", "row", "col"),
            P("section", "col", "row"),
            P("section", "row"),
        ),
        out_specs=(
            P("section", "row", "col"),
            P("section", "col", "row"),
            P("section", "row"),
            P("section", "col", "row"),
        ),
        check_vma=False,
    )
```

```python
import functools

import jax
import jax.numpy as jnp
from jax import lax
from jax.experimental import pallas as pl
from jax.experimental.pallas import tpu as pltpu
from jax.sharding import PartitionSpec as P

epsilon = 1e-06
half_root = 0.7071067811865476
density_factor = 0.3989422804014327

chunk_rows = (64, 64)
vmem_bytes = 60 * 1024 * 1024


def along_x(block, step):
    return lax.ppermute(block, "row", [(i, (i + step) % 4) for i in range(4)])


def along_z(block, step):
    route = [(j, j // 4 * 4 + (j % 4 + step) % 4) for j in range(8)]
    return lax.ppermute(block, "col", route)


def along_y(block):
    return lax.ppermute(block, "col", [(j, (j + 4) % 8) for j in range(8)])


def to_layer_before(block):
    return lax.ppermute(block, "section", [(i, i - 1) for i in range(1, 4)])


def gelu_parts(values):
    cumulative = 0.5 * (1.0 + lax.erf(values * half_root))
    density = jnp.exp(-0.5 * values * values) * density_factor
    return (values * cumulative, cumulative + values * density)


def dot_trans(left, right):
    return lax.dot_general(
        left, right, (((1,), (1,)), ((), ())), preferred_element_type=jnp.float32
    )


def trans_dot(left, right):
    return lax.dot_general(
        left, right, (((0,), (0,)), ((), ())), preferred_element_type=jnp.float32
    )


def whole(shape):
    return pl.BlockSpec(shape, lambda n, *_: (0,) * len(shape))


def columns(rows, width):
    return pl.BlockSpec((rows, width), lambda n, *_: (0, n))


def hidden_kernel(spans, tile, after, places, *refs):
    def source(pieces, block, rows):
        return pieces[block], 0

    def give(outputs, product, rows):
        own, to_right, to_left, right_top, left_bottom = outputs
        own[...] = product[: 2 * rows]
        right_top[...] = product[2 * rows : 3 * rows]
        to_right[rows:, :] = product[3 * rows : 4 * rows]
        to_right[:rows, :] = product[4 * rows : 5 * rows]
        to_left[rows:, :] = product[5 * rows : 6 * rows]
        to_left[:rows, :] = product[6 * rows : 7 * rows]
        left_bottom[...] = product[7 * rows :]

    tiled_products(spans, tile, 8, after, places, refs, source, give)


def normed_kernel(spans, tile, after, places, *refs):
    def source(pieces, block, rows):
        return pieces[block // 2], block % 2 * rows

    def give(outputs, product, rows):
        mine, to_up, to_down, up_same, down_other = outputs
        block = lambda place: product[place * rows : (place + 1) * rows]
        mine[:rows, :] = block(0)
        up_same[...] = block(1)
        to_up[:rows, :] = block(2)
        to_down[:rows, :] = block(3)
        mine[rows:, :] = block(4)
        to_up[rows:, :] = block(5)
        to_down[rows:, :] = block(6)
        down_other[...] = block(7)

    tiled_products(spans, tile, 4, after, places, refs, source, give)


def tiled_products(spans, tile, count, after, places, refs, source, give):
    chunks = len(spans)
    pieces, weight, refs = refs[:count], refs[count], refs[count + 1 + after :]
    kept, outputs = refs[:chunks], refs[chunks : 6 * chunks]
    held, arrived, fetched, saved = refs[6 * chunks :]
    step = pl.program_id(0)

    def weight_copy(index):
        place = pl.ds(index * tile, tile)
        return pltpu.make_async_copy(
            weight.at[place, :], held.at[place, :], fetched.at[index]
        )

    tiles = weight.shape[0] // tile
    bases, base = [], weight.shape[0]
    for _, rows in spans:
        bases.append(base)
        base += 8 * rows

    def save_copy(index):
        return pltpu.make_async_copy(
            held.at[pl.ds(bases[index], 8 * spans[index][1]), :], kept[index], saved.at[index]
        )

    @pl.when(step == 0)
    def _():
        copies = []
        for (first, rows), base in zip(spans, bases):
            for block in range(8):
                piece, offset = source(pieces, block, rows)
                start = pl.multiple_of(base + places[block] * rows, 16)
                copies.append(
                    pltpu.make_async_copy(
                        piece.at[pl.ds(first + offset, rows), :],
                        held.at[pl.ds(start, rows), :],
                        arrived.at[len(copies)],
                    )
                )
        for copy in copies:
            copy.start()
        for index in range(tiles):
            weight_copy(index).start()
        for copy in copies:
            copy.wait()
        for index in range(chunks):
            save_copy(index).start()

    for index in range(tiles):

        @pl.when(step == index)
        def _():
            weight_copy(index).wait()

    part = held[pl.ds(pl.multiple_of(step * tile, tile), tile), :]
    for index, (_, rows) in enumerate(spans):
        rhs = held[bases[index] : bases[index] + 8 * rows, :]
        give(outputs[5 * index : 5 * index + 5], dot_trans(rhs, part), rows)

    @pl.when(step == tiles - 1)
    def _():
        for index in range(chunks):
            save_copy(index).wait()


def parts_of(kernel, places, pieces, weight, spans, after=(), tile=256):
    width, depth = weight.shape
    rows = sum(8 * r for _, r in spans)
    chunks = len(spans)
    heights = [h for _, r in spans for h in (2 * r, 2 * r, 2 * r, r, r)]
    results = pl.pallas_call(
        functools.partial(kernel, spans, tile, len(after)),
        grid_spec=pltpu.PrefetchScalarGridSpec(
            num_scalar_prefetch=1,
            grid=(width // tile,),
            in_specs=[pl.BlockSpec(memory_space=pl.ANY)] * (len(pieces) + 1 + len(after)),
            out_specs=[pl.BlockSpec(memory_space=pl.ANY)] * chunks
            + [columns(h, tile) for h in heights],
            scratch_shapes=[
                pltpu.VMEM((width + rows, depth), jnp.bfloat16),
                pltpu.SemaphoreType.DMA((8 * chunks,)),
                pltpu.SemaphoreType.DMA((width // tile,)),
                pltpu.SemaphoreType.DMA((chunks,)),
            ],
        ),
        out_shape=[jax.ShapeDtypeStruct((8 * r, depth), jnp.bfloat16) for _, r in spans]
        + [jax.ShapeDtypeStruct((h, width), jnp.float32) for h in heights],
        compiler_params=pltpu.CompilerParams(vmem_limit_bytes=vmem_bytes),
        cost_estimate=pl.CostEstimate(
            flops=2 * rows * depth * width,
            bytes_accessed=2 * width * depth + 4 * rows * depth + 4 * rows * width,
            transcendentals=0,
        ),
    )(places, *pieces, weight, *after)
    return results[:chunks], [results[chunks + 5 * i : chunks + 5 * i + 5] for i in range(chunks)]


def weight_kernel(cuts, count, places, *refs):
    pieces, chunks = refs[:count], refs[count : count + len(cuts)]
    result, held = refs[-2:]
    total = None
    for chunk, cut in zip(chunks, cuts):
        at = 0
        for place, (piece, first, rows) in enumerate(cut):
            if count == 1:
                first = pl.multiple_of(places[place] + first, rows)
            held[at : at + rows, :] = pieces[piece][pl.ds(first, rows), :]
            at += rows
        term = trans_dot(held[:at, :], chunk[...])
        total = term if total is None else total + term
    result[0] = total.astype(result.dtype)


def weight_grad(places, pieces, cuts, chunks, after=(), tile=256):
    height = pieces[0].shape[1]
    width = chunks[0].shape[1]
    sizes = [chunk.shape[0] for chunk in chunks]
    return pl.pallas_call(
        functools.partial(weight_kernel, cuts, len(pieces)),
        grid_spec=pltpu.PrefetchScalarGridSpec(
            num_scalar_prefetch=1,
            grid=(height // tile,),
            in_specs=[columns(piece.shape[0], tile) for piece in pieces]
            + [whole(chunk.shape) for chunk in chunks]
            + [pl.BlockSpec(memory_space=pl.ANY)] * len(after),
            out_specs=pl.BlockSpec((1, tile, width), lambda n, *_: (0, n, 0)),
            scratch_shapes=[pltpu.VMEM((max(sizes), tile), jnp.bfloat16)],
        ),
        out_shape=jax.ShapeDtypeStruct((1, height, width), jnp.bfloat16),
        compiler_params=pltpu.CompilerParams(vmem_limit_bytes=vmem_bytes),
        cost_estimate=pl.CostEstimate(
            flops=2 * sum(sizes) * height * width,
            bytes_accessed=2 * (sum(sizes) * (height + width) + height * width),
            transcendentals=0,
        ),
    )(places, *pieces, *chunks, *after)


def hold(block, *after):
    return lax.optimization_barrier((block,) + after)


def start_col(block):
    return along_z(block, -1), along_z(block, 2), along_z(block, 1), along_y(block)


def finish_col(block, from_up, far, from_down, beside):
    beside_up, beside_down = along_z(beside, -1), along_z(beside, 1)
    beside_far = along_y(far)
    return [block, from_up, far, from_down, beside, beside_up, beside_far, beside_down]


def gather_row(block):
    return [block, along_x(block, -1), along_x(block, 2), along_x(block, 1)]


def sum_row(block):
    return (block + along_x(block, 2)) + (along_x(block, 1) + along_x(block, -1))


def sum_col(block):
    block = (block + along_z(block, 2)) + (along_z(block, 1) + along_z(block, -1))
    return block + along_y(block)


def ring_start(along, to_next, to_last):
    return along(to_next, 1), along(to_last, -1)


def ring_go_on(along, rows, next_first, last_second, from_last, from_next):
    first = along(next_first + from_last[:rows], 1)
    second = along(last_second + from_next[rows:], -1)
    return first, second


def ring_sums(rows, own, from_last, from_next, first, second):
    return (own[:rows] + from_next[:rows]) + first, (own[rows:] + from_last[rows:]) + second


def local(inputs, cotangent, stashed, weight_in, weight_out, norm_gain):
    local_input = inputs[0]
    upstream = cotangent[0]
    hidden_pre = stashed[0]
    first_weight = weight_in[0]
    second_weight = weight_out[0]
    gains = norm_gain[0]
    width = gains.shape[0]
    feature_count = width * lax.axis_size("row")
    tokens = upstream.shape[0]
    row, col = lax.axis_index("row"), lax.axis_index("col")
    step = jnp.arange(8, dtype=jnp.int32)
    owner = (col // 4 + step // 4) % 2 * 4 + (col + step) % 4
    order = (owner // 2 - row + 4) % 4 * 2 + owner % 2
    ring_owner = (row + step // 2) % 4 * 2 + step % 2
    ring_order = (ring_owner // 4 + col // 4) % 2 * 4 + (ring_owner - col + 8) % 4

    spans, start = [], 0
    for rows in chunk_rows:
        spans.append((start, rows))
        start += rows

    begun = start_col(upstream)
    activated = gelu_parts(hidden_pre.astype(jnp.float32))[0].astype(jnp.bfloat16)
    values = local_input.astype(jnp.float32)
    sums = jnp.stack([jnp.sum(values, axis=1), jnp.sum(values * values, axis=1)])
    beside, activated = hold(begun[-1], activated)
    begun = begun[:-1] + (beside,)
    activ_right, activ_left = along_x(activated, -1), along_x(activated, 1)
    cot_pieces = finish_col(upstream, *begun)

    cot_chunks, parts = parts_of(
        hidden_kernel, order, cot_pieces, second_weight, spans, (activ_right, activ_left)
    )
    first_own, to_right, to_left, *first_near = parts[0]
    first_begun = ring_start(along_x, to_right, to_left)

    sums, first_own = hold(sums, first_own)
    sums = sum_row(sums)
    average = sums[0] / feature_count
    inv_scale = lax.rsqrt(sums[1] / feature_count - average * average + epsilon)
    standard = (values - average[:, None]) * inv_scale[:, None]
    normed = (standard * gains).astype(jnp.bfloat16)
    normed_full = lax.all_to_all(
        jnp.broadcast_to(normed[None], (8,) + normed.shape), "col", 0, 0
    ).reshape(8 * tokens, width)

    def deltas_of(span, top, bottom):
        s, r = span
        slopes = [
            gelu_parts(hidden_pre[first : first + r].astype(jnp.float32))[1]
            for first in (s, tokens + s)
        ]
        return jnp.concatenate([top * slopes[0], bottom * slopes[1]]).astype(jnp.bfloat16)

    second_own, to_right, to_left, *second_near = parts[1]
    *first_begun, to_right, to_left = hold(*first_begun, to_right, to_left)
    first_rest = ring_go_on(along_x, spans[0][1], *first_near, *first_begun)
    second_begun = ring_start(along_x, to_right, to_left)
    deltas = deltas_of(spans[0], *ring_sums(spans[0][1], first_own, *first_begun, *first_rest))
    first_pieces = gather_row(deltas)
    second_rest = ring_go_on(along_x, spans[1][1], *second_near, *second_begun)
    *second_rest, deltas, normed_full = hold(*second_rest, deltas, normed_full)
    first_pieces[0] = deltas
    deltas = deltas_of(spans[1], *ring_sums(spans[1][1], second_own, *second_begun, *second_rest))
    second_pieces = gather_row(deltas)

    (first_deltas,), (parts,) = parts_of(
        normed_kernel, ring_order, first_pieces, first_weight, [(0, spans[0][1])]
    )
    first_own, to_up, to_down, *first_near = parts
    first_begun = ring_start(along_z, to_up, to_down)
    (second_deltas,), (parts,) = parts_of(
        normed_kernel, ring_order, second_pieces, first_weight, [(0, spans[1][1])]
    )
    second_own, to_up, to_down, *second_near = parts
    second_begun = ring_start(along_z, to_up, to_down)

    activ_left, activ_right, second_deltas = hold(activ_left, activ_right, second_deltas)
    activ_top = along_x(activ_left[:tokens], 1)
    activ_bottom = along_x(activ_right[tokens:], -1)
    activ_pieces = [activated, activ_right, activ_top, activ_bottom, activ_left]

    activ_cuts, normed_cuts = [], []
    for s, r in spans:
        activ_cuts.append(
            [
                (0, s, r),
                (0, tokens + s, r),
                (1, s, r),
                (1, tokens + s, r),
                (2, s, r),
                (3, s, r),
                (4, s, r),
                (4, tokens + s, r),
            ]
        )
        normed_cuts.append([(0, s, r)] * 8)
    in_grad = weight_grad(
        owner * tokens, [normed_full], normed_cuts, [first_deltas, second_deltas]
    )
    out_grad = weight_grad(owner, activ_pieces, activ_cuts, cot_chunks)

    first_rest = ring_go_on(along_z, spans[0][1], *first_near, *first_begun)
    *second_begun, in_grad = hold(*second_begun, in_grad)
    second_rest = ring_go_on(along_z, spans[1][1], *second_near, *second_begun)
    same, other = ring_sums(spans[0][1], first_own, *first_begun, *first_rest)
    grads = [same + along_y(other)]
    *second_rest, out_grad = hold(*second_rest, out_grad)
    same, other = ring_sums(spans[1][1], second_own, *second_begun, *second_rest)
    grads.append(same + along_y(other))

    normed_grad = jnp.concatenate(grads)
    gain_part = jnp.sum(normed_grad * standard, axis=0)
    scaled_grad = normed_grad * gains
    means = jnp.stack([jnp.sum(scaled_grad, axis=1), jnp.sum(scaled_grad * standard, axis=1)])
    means = sum_row(means) / feature_count
    means, gain_part = hold(means, gain_part)
    result_grad = upstream.astype(jnp.float32) + inv_scale[:, None] * (
        scaled_grad - means[0][:, None] - standard * means[1][:, None]
    )
    received = to_layer_before(result_grad.astype(jnp.bfloat16))
    gain_grad = sum_col(gain_part[None])
    return (in_grad, out_grad, gain_grad, received[None])


def solution(mesh):
    return jax.shard_map(
        local,
        mesh=mesh,
        in_specs=(
            P("section", "col", "row"),
            P("section", "col", "row"),
            P("section", "row", "col"),
            P("section", "row", "col"),
            P("section", "col", "row"),
            P("section", "row"),
        ),
        out_specs=(
            P("section", "row", "col"),
            P("section", "col", "row"),
            P("section", "row"),
            P("section", "col", "row"),
        ),
        check_vma=False,
    )
```

```python
import functools

import jax
import jax.numpy as jnp
from jax import lax
from jax.experimental import pallas as pl
from jax.experimental.pallas import tpu as pltpu
from jax.sharding import PartitionSpec as P

epsilon = 1e-06
half_root = 0.7071067811865476
density_factor = 0.3989422804014327

chunk_rows = (64, 64)
vmem_bytes = 60 * 1024 * 1024


def along_x(block, step):
    return lax.ppermute(block, "row", [(i, (i + step) % 4) for i in range(4)])


def along_z(block, step):
    route = [(j, j // 4 * 4 + (j % 4 + step) % 4) for j in range(8)]
    return lax.ppermute(block, "col", route)


def along_y(block):
    return lax.ppermute(block, "col", [(j, (j + 4) % 8) for j in range(8)])


def to_layer_before(block):
    return lax.ppermute(block, "section", [(i, i - 1) for i in range(1, 4)])


def gelu_parts(values):
    cumulative = 0.5 * (1.0 + lax.erf(values * half_root))
    density = jnp.exp(-0.5 * values * values) * density_factor
    return (values * cumulative, cumulative + values * density)


def dot_trans(left, right):
    return lax.dot_general(
        left, right, (((1,), (1,)), ((), ())), preferred_element_type=jnp.float32
    )


def trans_dot(left, right):
    return lax.dot_general(
        left, right, (((0,), (0,)), ((), ())), preferred_element_type=jnp.float32
    )


def whole(shape):
    return pl.BlockSpec(shape, lambda n, *_: (0,) * len(shape))


def columns(rows, width):
    return pl.BlockSpec((rows, width), lambda n, *_: (0, n))


def hidden_kernel(spans, tile, after, places, *refs):
    def source(pieces, block, rows):
        return pieces[block], 0

    def give(outputs, product, rows):
        own, to_right, to_left, right_top, left_bottom = outputs
        own[...] = product[: 2 * rows]
        right_top[...] = product[2 * rows : 3 * rows]
        to_right[rows:, :] = product[3 * rows : 4 * rows]
        to_right[:rows, :] = product[4 * rows : 5 * rows]
        to_left[rows:, :] = product[5 * rows : 6 * rows]
        to_left[:rows, :] = product[6 * rows : 7 * rows]
        left_bottom[...] = product[7 * rows :]

    tiled_products(spans, tile, 8, after, places, refs, source, give)


def normed_kernel(spans, tile, after, places, *refs):
    def source(pieces, block, rows):
        return pieces[block // 2], block % 2 * rows

    def give(outputs, product, rows):
        mine, to_up, to_down, up_same, down_other = outputs
        block = lambda place: product[place * rows : (place + 1) * rows]
        mine[:rows, :] = block(0)
        up_same[...] = block(1)
        to_up[:rows, :] = block(2)
        to_down[:rows, :] = block(3)
        mine[rows:, :] = block(4)
        to_up[rows:, :] = block(5)
        to_down[rows:, :] = block(6)
        down_other[...] = block(7)

    tiled_products(spans, tile, 4, after, places, refs, source, give)


def tiled_products(spans, tile, count, after, places, refs, source, give):
    chunks = len(spans)
    pieces, weight, refs = refs[:count], refs[count], refs[count + 1 + after :]
    kept, outputs = refs[:chunks], refs[chunks : 6 * chunks]
    held, arrived, fetched, saved = refs[6 * chunks :]
    step = pl.program_id(0)

    def weight_copy(index):
        place = pl.ds(index * tile, tile)
        return pltpu.make_async_copy(
            weight.at[place, :], held.at[place, :], fetched.at[index]
        )

    tiles = weight.shape[0] // tile
    bases, base = [], weight.shape[0]
    for _, rows in spans:
        bases.append(base)
        base += 8 * rows

    def save_copy(index):
        return pltpu.make_async_copy(
            held.at[pl.ds(bases[index], 8 * spans[index][1]), :], kept[index], saved.at[index]
        )

    @pl.when(step == 0)
    def _():
        copies = []
        for (first, rows), base in zip(spans, bases):
            for block in range(8):
                piece, offset = source(pieces, block, rows)
                start = pl.multiple_of(base + places[block] * rows, 16)
                copies.append(
                    pltpu.make_async_copy(
                        piece.at[pl.ds(first + offset, rows), :],
                        held.at[pl.ds(start, rows), :],
                        arrived.at[len(copies)],
                    )
                )
        for copy in copies:
            copy.start()
        for index in range(tiles):
            weight_copy(index).start()
        for copy in copies:
            copy.wait()
        for index in range(chunks):
            save_copy(index).start()

    for index in range(tiles):

        @pl.when(step == index)
        def _():
            weight_copy(index).wait()

    part = held[pl.ds(pl.multiple_of(step * tile, tile), tile), :]
    for index, (_, rows) in enumerate(spans):
        rhs = held[bases[index] : bases[index] + 8 * rows, :]
        give(outputs[5 * index : 5 * index + 5], dot_trans(rhs, part), rows)

    @pl.when(step == tiles - 1)
    def _():
        for index in range(chunks):
            save_copy(index).wait()


def parts_of(kernel, places, pieces, weight, spans, after=(), tile=512):
    width, depth = weight.shape
    rows = sum(8 * r for _, r in spans)
    chunks = len(spans)
    heights = [h for _, r in spans for h in (2 * r, 2 * r, 2 * r, r, r)]
    results = pl.pallas_call(
        functools.partial(kernel, spans, tile, len(after)),
        grid_spec=pltpu.PrefetchScalarGridSpec(
            num_scalar_prefetch=1,
            grid=(width // tile,),
            in_specs=[pl.BlockSpec(memory_space=pl.ANY)] * (len(pieces) + 1 + len(after)),
            out_specs=[pl.BlockSpec(memory_space=pl.ANY)] * chunks
            + [columns(h, tile) for h in heights],
            scratch_shapes=[
                pltpu.VMEM((width + rows, depth), jnp.bfloat16),
                pltpu.SemaphoreType.DMA((8 * chunks,)),
                pltpu.SemaphoreType.DMA((width // tile,)),
                pltpu.SemaphoreType.DMA((chunks,)),
            ],
        ),
        out_shape=[jax.ShapeDtypeStruct((8 * r, depth), jnp.bfloat16) for _, r in spans]
        + [jax.ShapeDtypeStruct((h, width), jnp.float32) for h in heights],
        compiler_params=pltpu.CompilerParams(vmem_limit_bytes=vmem_bytes),
        cost_estimate=pl.CostEstimate(
            flops=2 * rows * depth * width,
            bytes_accessed=2 * width * depth + 4 * rows * depth + 4 * rows * width,
            transcendentals=0,
        ),
    )(places, *pieces, weight, *after)
    return results[:chunks], [results[chunks + 5 * i : chunks + 5 * i + 5] for i in range(chunks)]


def weight_kernel(cuts, count, places, *refs):
    pieces, chunks = refs[:count], refs[count : count + len(cuts)]
    result, held = refs[-2:]
    total = None
    for chunk, cut in zip(chunks, cuts):
        at = 0
        for place, (piece, first, rows) in enumerate(cut):
            if count == 1:
                first = pl.multiple_of(places[place] + first, rows)
            held[at : at + rows, :] = pieces[piece][pl.ds(first, rows), :]
            at += rows
        term = trans_dot(held[:at, :], chunk[...])
        total = term if total is None else total + term
    result[0] = total.astype(result.dtype)


def weight_grad(places, pieces, cuts, chunks, after=(), tile=512):
    height = pieces[0].shape[1]
    width = chunks[0].shape[1]
    sizes = [chunk.shape[0] for chunk in chunks]
    return pl.pallas_call(
        functools.partial(weight_kernel, cuts, len(pieces)),
        grid_spec=pltpu.PrefetchScalarGridSpec(
            num_scalar_prefetch=1,
            grid=(height // tile,),
            in_specs=[columns(piece.shape[0], tile) for piece in pieces]
            + [whole(chunk.shape) for chunk in chunks]
            + [pl.BlockSpec(memory_space=pl.ANY)] * len(after),
            out_specs=pl.BlockSpec((1, tile, width), lambda n, *_: (0, n, 0)),
            scratch_shapes=[pltpu.VMEM((max(sizes), tile), jnp.bfloat16)],
        ),
        out_shape=jax.ShapeDtypeStruct((1, height, width), jnp.bfloat16),
        compiler_params=pltpu.CompilerParams(vmem_limit_bytes=vmem_bytes),
        cost_estimate=pl.CostEstimate(
            flops=2 * sum(sizes) * height * width,
            bytes_accessed=2 * (sum(sizes) * (height + width) + height * width),
            transcendentals=0,
        ),
    )(places, *pieces, *chunks, *after)


def hold(block, *after):
    return lax.optimization_barrier((block,) + after)


def start_col(block):
    return along_z(block, -1), along_z(block, 2), along_z(block, 1), along_y(block)


def finish_col(block, from_up, far, from_down, beside):
    beside_up, beside_down = along_z(beside, -1), along_z(beside, 1)
    beside_far = along_y(far)
    return [block, from_up, far, from_down, beside, beside_up, beside_far, beside_down]


def gather_row(block):
    return [block, along_x(block, -1), along_x(block, 2), along_x(block, 1)]


def sum_row(block):
    return (block + along_x(block, 2)) + (along_x(block, 1) + along_x(block, -1))


def sum_col(block):
    block = (block + along_z(block, 2)) + (along_z(block, 1) + along_z(block, -1))
    return block + along_y(block)


def ring_start(along, to_next, to_last):
    return along(to_next, 1), along(to_last, -1)


def ring_go_on(along, rows, next_first, last_second, from_last, from_next):
    first = along(next_first + from_last[:rows], 1)
    second = along(last_second + from_next[rows:], -1)
    return first, second


def ring_sums(rows, own, from_last, from_next, first, second):
    return (own[:rows] + from_next[:rows]) + first, (own[rows:] + from_last[rows:]) + second


def local(inputs, cotangent, stashed, weight_in, weight_out, norm_gain):
    local_input = inputs[0]
    upstream = cotangent[0]
    hidden_pre = stashed[0]
    first_weight = weight_in[0]
    second_weight = weight_out[0]
    gains = norm_gain[0]
    width = gains.shape[0]
    feature_count = width * lax.axis_size("row")
    tokens = upstream.shape[0]
    row, col = lax.axis_index("row"), lax.axis_index("col")
    step = jnp.arange(8, dtype=jnp.int32)
    owner = (col // 4 + step // 4) % 2 * 4 + (col + step) % 4
    order = (owner // 2 - row + 4) % 4 * 2 + owner % 2
    ring_owner = (row + step // 2) % 4 * 2 + step % 2
    ring_order = (ring_owner // 4 + col // 4) % 2 * 4 + (ring_owner - col + 8) % 4

    spans, start = [], 0
    for rows in chunk_rows:
        spans.append((start, rows))
        start += rows

    begun = start_col(upstream)
    activated = gelu_parts(hidden_pre.astype(jnp.float32))[0].astype(jnp.bfloat16)
    values = local_input.astype(jnp.float32)
    sums = jnp.stack([jnp.sum(values, axis=1), jnp.sum(values * values, axis=1)])
    beside, activated = hold(begun[-1], activated)
    begun = begun[:-1] + (beside,)
    activ_right, activ_left = along_x(activated, -1), along_x(activated, 1)
    cot_pieces = finish_col(upstream, *begun)

    cot_chunks, parts = parts_of(
        hidden_kernel, order, cot_pieces, second_weight, spans, (activ_right, activ_left)
    )
    first_own, to_right, to_left, *first_near = parts[0]
    first_begun = ring_start(along_x, to_right, to_left)

    sums, first_own = hold(sums, first_own)
    sums = sum_row(sums)
    average = sums[0] / feature_count
    inv_scale = lax.rsqrt(sums[1] / feature_count - average * average + epsilon)
    standard = (values - average[:, None]) * inv_scale[:, None]
    normed = (standard * gains).astype(jnp.bfloat16)
    normed_full = lax.all_to_all(
        jnp.broadcast_to(normed[None], (8,) + normed.shape), "col", 0, 0
    ).reshape(8 * tokens, width)

    def deltas_of(span, top, bottom):
        s, r = span
        slopes = [
            gelu_parts(hidden_pre[first : first + r].astype(jnp.float32))[1]
            for first in (s, tokens + s)
        ]
        return jnp.concatenate([top * slopes[0], bottom * slopes[1]]).astype(jnp.bfloat16)

    second_own, to_right, to_left, *second_near = parts[1]
    *first_begun, to_right, to_left = hold(*first_begun, to_right, to_left)
    first_rest = ring_go_on(along_x, spans[0][1], *first_near, *first_begun)
    second_begun = ring_start(along_x, to_right, to_left)
    deltas = deltas_of(spans[0], *ring_sums(spans[0][1], first_own, *first_begun, *first_rest))
    first_pieces = gather_row(deltas)
    second_rest = ring_go_on(along_x, spans[1][1], *second_near, *second_begun)
    *second_rest, deltas, normed_full = hold(*second_rest, deltas, normed_full)
    first_pieces[0] = deltas
    deltas = deltas_of(spans[1], *ring_sums(spans[1][1], second_own, *second_begun, *second_rest))
    second_pieces = gather_row(deltas)

    (first_deltas,), (parts,) = parts_of(
        normed_kernel, ring_order, first_pieces, first_weight, [(0, spans[0][1])]
    )
    first_own, to_up, to_down, *first_near = parts
    first_begun = ring_start(along_z, to_up, to_down)
    (second_deltas,), (parts,) = parts_of(
        normed_kernel, ring_order, second_pieces, first_weight, [(0, spans[1][1])]
    )
    second_own, to_up, to_down, *second_near = parts
    second_begun = ring_start(along_z, to_up, to_down)

    activ_left, activ_right, second_deltas = hold(activ_left, activ_right, second_deltas)
    activ_top = along_x(activ_left[:tokens], 1)
    activ_bottom = along_x(activ_right[tokens:], -1)
    activ_pieces = [activated, activ_right, activ_top, activ_bottom, activ_left]

    activ_cuts, normed_cuts = [], []
    for s, r in spans:
        activ_cuts.append(
            [
                (0, s, r),
                (0, tokens + s, r),
                (1, s, r),
                (1, tokens + s, r),
                (2, s, r),
                (3, s, r),
                (4, s, r),
                (4, tokens + s, r),
            ]
        )
        normed_cuts.append([(0, s, r)] * 8)
    in_grad = weight_grad(
        owner * tokens, [normed_full], normed_cuts, [first_deltas, second_deltas]
    )
    out_grad = weight_grad(owner, activ_pieces, activ_cuts, cot_chunks)

    first_rest = ring_go_on(along_z, spans[0][1], *first_near, *first_begun)
    *second_begun, in_grad = hold(*second_begun, in_grad)
    second_rest = ring_go_on(along_z, spans[1][1], *second_near, *second_begun)
    same, other = ring_sums(spans[0][1], first_own, *first_begun, *first_rest)
    grads = [same + along_y(other)]
    *second_rest, out_grad = hold(*second_rest, out_grad)
    same, other = ring_sums(spans[1][1], second_own, *second_begun, *second_rest)
    grads.append(same + along_y(other))

    normed_grad = jnp.concatenate(grads)
    gain_part = jnp.sum(normed_grad * standard, axis=0)
    scaled_grad = normed_grad * gains
    means = jnp.stack([jnp.sum(scaled_grad, axis=1), jnp.sum(scaled_grad * standard, axis=1)])
    means = sum_row(means) / feature_count
    means, gain_part = hold(means, gain_part)
    result_grad = upstream.astype(jnp.float32) + inv_scale[:, None] * (
        scaled_grad - means[0][:, None] - standard * means[1][:, None]
    )
    received = to_layer_before(result_grad.astype(jnp.bfloat16))
    gain_grad = sum_col(gain_part[None])
    return (in_grad, out_grad, gain_grad, received[None])


def solution(mesh):
    return jax.shard_map(
        local,
        mesh=mesh,
        in_specs=(
            P("section", "col", "row"),
            P("section", "col", "row"),
            P("section", "row", "col"),
            P("section", "row", "col"),
            P("section", "col", "row"),
            P("section", "row"),
        ),
        out_specs=(
            P("section", "row", "col"),
            P("section", "col", "row"),
            P("section", "row"),
            P("section", "col", "row"),
        ),
        check_vma=False,
    )
```
